512 devices in a mesh: ex: 16 (over y_lo, z), feat: 32 (over x, y_hi, core).
Axes of the slice: x: 4, y: 8 (y_hi: 4, y_lo: 2; y = y_hi * 2 + y_lo), z: 8, core: 2. Of those that a mesh axis runs over, the one named last changes fastest.
Arguments:
- grads: float32 [4096, 8192], P('ex', 'feat'), may hold values from -6 to 6
- second_moment: float32 [8192], P('feat'), may hold values from 0.0001 to 0.01
Outputs:
- similarity: float32 [4096, 4096], P(('ex', 'feat'))
The draws below stay inside these ranges and needn't reach their ends.
All inputs are finite; a program needn't handle non-finite values.
Results may differ from the reference program's by a relative error of at most 0.000096.
Values sent between devices are 32-bit elements; how exact they have to be, the bound alone decides.
No kernel may reach another device: no remote copies, remote signals or barrier semaphores. Data moves between devices by JAX's collectives and lax.ppermute only.
A program may use at most 64 MiB of HBM per device.

```python
import math
import jax
import jax.numpy as jnp
from jax import lax

F = 8192
N = 4096


def block_scale(rng, dims, split, smallest, top_value):
    loudness, own = 1.0, jax.random.fold_in(rng, 6)
    for axis_at, shards_of in split:
        steps = jnp.exp(jax.random.uniform(jax.random.fold_in(own, axis_at), (shards_of,), jnp.float32, smallest / len(split), top_value / len(split)))
        loudness = loudness * jnp.repeat(steps, dims[axis_at] // shards_of).reshape([-1 if axis == axis_at else 1 for axis in range(len(dims))])
    return loudness


def centred(rng, shape, width, most, pieces=(), kind=jnp.bfloat16):
    array = jax.random.normal(rng, shape, jnp.float32) * width
    if len(pieces) > 0:
        array = block_scale(rng, shape, pieces, -0.22, 0.18) * array
    return jnp.clip(array, min=-most, max=most).astype(kind)


def setup_inputs(seed: int = 0) -> dict:
    keys = jax.random.split(jax.random.key(seed), 3)
    grads = centred(keys[0], (N, F), 1.0, 6.0, ((0, 16), (1, 32)), jnp.float32)
    second_moment = jnp.clip(jnp.exp(math.log(0.01) - 4.6051702 * jax.random.uniform(keys[1], (F,), jnp.float32) ** block_scale(keys[1], (F,), ((0, 32),), -0.2, 0.2)), 0.0001, 0.01)
    return dict(grads=grads, second_moment=second_moment)


def reference(grads, second_moment):
    scaled = grads / (jnp.sqrt(second_moment) + 1e-08)[None, :]
    row_sq = lax.optimization_barrier(jnp.sum(scaled * scaled, axis=1))
    unit = scaled / jnp.sqrt(row_sq + 1e-06)[:, None]
    return jnp.dot(unit, unit.T, precision=lax.Precision.HIGHEST, preferred_element_type=jnp.float32)
```

```python
import jax
import jax.numpy as jnp
from jax import lax
from jax.sharding import PartitionSpec as P

XS, YH, YL, ZS, CS = 4, 4, 2, 8, 2
YS = YH * YL
FEAT = XS * YH * CS
AXES = ("ex", "feat")


def device_at(x, y, z, c):
    return ((y % YL) * ZS + z) * FEAT + x * (YH * CS) + (y // YL) * CS + c


YH_GROUPS = [[x * (YH * CS) + yh * CS + c for yh in range(YH)] for x in range(XS) for c in range(CS)]
XY_GROUPS = [[device_at(x, y, z, c) for x in range(XS) for y in range(YS)]
             for z in range(ZS) for c in range(CS)]


def shift(value, move):
    pairs = []
    for x in range(XS):
        for y in range(YS):
            for z in range(ZS):
                for c in range(CS):
                    nx, ny, nz, nc = move(x, y, z, c)
                    pairs.append((device_at(x, y, z, c), device_at(nx % XS, ny % YS, nz % ZS, nc % CS)))
    return lax.ppermute(value, AXES, pairs)


def rings(piece):
    along_y = {0: piece}
    along_z = {0: piece}
    for step in range(1, 5):
        for way in (1, -1):
            if step == 4 and way < 0:
                continue
            at, before = way * step, way * (step - 1)
            turn = lambda c: -way if c == 0 else way
            along_y[at] = shift(along_y[before], lambda x, y, z, c: (x, y + turn(c), z, c))
            along_z[at] = shift(along_z[before], lambda x, y, z, c: (x, y, z + turn(c), c))
    return along_y, along_z


def placed(along_y, along_z, y, z, sign):
    whole = jnp.zeros((16,) + along_y[0].shape, jnp.float32)
    for t in along_y:
        whole = lax.dynamic_update_slice(whole, along_y[t][None], ((y + sign * t) % 8, 0, 0))
        whole = lax.dynamic_update_slice(whole, along_z[t][None], (8 + (z + sign * t) % 8, 0, 0))
    whole = whole.reshape(2, 512, -1)
    return whole[0], whole[1]


def shards(grads, second_moment):
    ex, feat = lax.axis_index("ex"), lax.axis_index("feat")
    z, y_lo = ex % ZS, ex // ZS
    y_hi, core = (feat // CS) % YH, feat % CS
    y = y_hi * YL + y_lo
    sign = 1 - 2 * core

    scaled = grads * (1.0 / (jnp.sqrt(second_moment) + 1e-08))[None, :]
    swapped = lax.all_to_all(scaled.reshape(YH, 64, 256), "feat", 0, 0, axis_index_groups=YH_GROUPS, tiled=True)
    piece = jnp.transpose(swapped, (1, 0, 2)).reshape(64, YH * 256)
    along_y, along_z = rings(piece)
    left, right = placed(along_y, along_z, y, z, sign)

    part = lax.dot_general(left, right, (((1,), (1,)), ((), ())), precision=lax.Precision.HIGH,
                           preferred_element_type=jnp.float32)
    sq = jnp.sum(right * right, axis=1)

    part = jnp.transpose(part.reshape(XS, YL, YH, CS, 8, 4, 128), (3, 0, 2, 1, 5, 4, 6)).reshape(CS, XS * YS, 4, 8, 128)
    sq = jnp.broadcast_to(jnp.pad(sq.reshape(4, 128), ((0, 4), (0, 0))), (CS, XS * YS, 1, 8, 128))
    part = jnp.concatenate([part, sq], axis=2)
    take = lambda i: lax.dynamic_index_in_dim(part, i, 0, keepdims=False)
    part = take(core) + shift(take(1 - core), lambda x, y, z, c: (x, y, z, c + 1))
    whole = lax.all_to_all(part, AXES, 0, 0, axis_index_groups=XY_GROUPS, tiled=True)
    whole = jnp.sum(whole.reshape(XS, YS, 5, 8, 128), axis=0)

    scale = lax.rsqrt(whole[:, 4, :4] + 1e-06)
    scale = jnp.transpose(scale.reshape(YH, YL, ZS, 64), (1, 2, 0, 3)).reshape(4096)
    out = whole[:, :4].reshape(YH, YL, 4, 8, 2, 64)
    out = jnp.transpose(out, (3, 1, 2, 4, 0, 5)).reshape(8, 4096)
    own = lax.dynamic_slice(scale, (ex * 256 + feat * 8,), (8,))
    return out * scale[None, :] * own[:, None]


def solution(mesh):
    return jax.shard_map(
        shards,
        mesh=mesh,
        in_specs=(P("ex", "feat"), P("feat")),
        out_specs=P(("ex", "feat"), None),
        check_vma=False,
    )
```

```python
import jax
import jax.numpy as jnp
from jax import lax
from jax.experimental import pallas as pl
from jax.experimental.pallas import tpu as pltpu
from jax.sharding import PartitionSpec as P

XS, YH, YL, ZS, CS = 4, 4, 2, 8, 2
YS = YH * YL
FEAT = XS * YH * CS
AXES = ("ex", "feat")
VMEM = pl.BlockSpec(memory_space=pltpu.VMEM)
SMEM = pl.BlockSpec(memory_space=pltpu.SMEM)
PARAMS = pltpu.CompilerParams(vmem_limit_bytes=32 * 1024 * 1024)


def device_at(x, y, z, c):
    return ((y % YL) * ZS + z) * FEAT + x * (YH * CS) + (y // YL) * CS + c


X_GROUPS = [[x * (YH * CS) + yh * CS + c for x in range(XS)] for yh in range(YH) for c in range(CS)]
LEFT_GROUPS = [[device_at(x, yh * YL + yl, z, c) for x in range(XS) for yl in range(YL)]
               for yh in range(YH) for z in range(ZS) for c in range(CS)]
XY_GROUPS = [[device_at(x, y, z, c) for x in range(XS) for y in range(YS)]
             for z in range(ZS) for c in range(CS)]


def shift(value, move):
    pairs = []
    for x in range(XS):
        for y in range(YS):
            for z in range(ZS):
                for c in range(CS):
                    nx, ny, nz, nc = move(x, y, z, c)
                    pairs.append((device_at(x, y, z, c), device_at(nx % XS, ny % YS, nz % ZS, nc % CS)))
    return lax.ppermute(value, AXES, pairs)


def ring(piece, at, sign):
    whole = lax.dynamic_update_slice(jnp.zeros((ZS,) + piece.shape, jnp.float32), piece[None], (at, 0, 0))
    ahead, behind = piece, piece
    for step in range(1, 5):
        ahead = shift(ahead, lambda x, y, z, c: (x, y, z + (-1 if c == 0 else 1), c))
        whole = lax.dynamic_update_slice(whole, ahead[None], ((at + sign * step) % ZS, 0, 0))
        if step < 4:
            behind = shift(behind, lambda x, y, z, c: (x, y, z + (1 if c == 0 else -1), c))
            whole = lax.dynamic_update_slice(whole, behind[None], ((at - sign * step) % ZS, 0, 0))
    return whole.reshape(-1, piece.shape[1])


def scale_kernel(grads_ref, moment_ref, scaled_ref, copies_ref):
    scaled = grads_ref[...] * (1.0 / (jnp.sqrt(moment_ref[...]) + 1e-08))
    scaled_ref[...] = scaled
    for i in range(XS * YL):
        copies_ref[i] = scaled


def scale(grads, second_moment):
    return pl.pallas_call(
        scale_kernel,
        out_shape=(jax.ShapeDtypeStruct((256, 256), jnp.float32),
                   jax.ShapeDtypeStruct((XS * YL, 256, 256), jnp.float32)),
        in_specs=[VMEM, VMEM],
        out_specs=(VMEM, VMEM),
        compiler_params=PARAMS,
        cost_estimate=pl.CostEstimate(flops=65536, bytes_accessed=2621440, transcendentals=256),
    )(grads, second_moment.reshape(1, 256))


def halves(value):
    high = value.astype(jnp.bfloat16)
    return high, (value - high.astype(jnp.float32)).astype(jnp.bfloat16)


def dot_t(left, right):
    return lax.dot_general(left, right, (((1,), (1,)), ((), ())), preferred_element_type=jnp.float32)


def product_kernel(core_ref, left_ref, right_ref, mine_ref, theirs_ref, total_ref):
    ones = jnp.ones((8, 256), jnp.bfloat16)
    sums = jnp.zeros((8, 512), jnp.float32)
    for x in range(XS):
        block = right_ref[:, x * 256:(x + 1) * 256]
        right_high, right_low = halves(block)
        square_high, square_low = halves(block * block)
        sums = sums + dot_t(ones, square_high) + dot_t(ones, square_low)
        for yl in range(YL):
            left_high, left_low = halves(left_ref[x * YL + yl])
            part = dot_t(left_high, right_high) + dot_t(left_high, right_low) + dot_t(left_low, right_high)
            if x == 0:
                total_ref[yl] = part
            else:
                total_ref[yl] += part
    row = lax.broadcasted_iota(jnp.int32, (8, 128), 0)
    tile = jnp.zeros((8, 128), jnp.float32)
    for q in range(4):
        tile = jnp.where(row == q, sums[:, q * 128:(q + 1) * 128], tile)

    def write(refs):
        for x in range(XS):
            for yh in range(YH):
                for yl in range(YL):
                    to = (x * YH + yh) * YL + yl
                    for c in range(CS):
                        at = x * 64 + yh * 16 + c * 8
                        for q in range(4):
                            refs[c][to, q] = total_ref[yl, at:at + 8, q * 128:(q + 1) * 128]
                        refs[c][to, 4] = tile

    @pl.when(core_ref[0] == 0)
    def _():
        write((mine_ref, theirs_ref))

    @pl.when(core_ref[0] == 1)
    def _():
        write((theirs_ref, mine_ref))


def product(core, left, right):
    message = jax.ShapeDtypeStruct((XS * YS, 5, 8, 128), jnp.float32)
    return pl.pallas_call(
        product_kernel,
        out_shape=(message, message),
        in_specs=[SMEM, VMEM, VMEM],
        out_specs=(VMEM, VMEM),
        scratch_shapes=[pltpu.VMEM((YL, 256, 512), jnp.float32)],
        compiler_params=PARAMS,
        cost_estimate=pl.CostEstimate(flops=3 * 2 * 512 * 512 * 1024, bytes_accessed=5505024, transcendentals=0),
    )(core.reshape(1), left, right)


def finish_kernel(place_ref, whole_ref, out_ref, scale_ref):
    row = lax.broadcasted_iota(jnp.int32, (8, 128), 0)
    lane = lax.broadcasted_iota(jnp.int32, (8, 128), 1)
    tiles = {}
    for x in range(XS):
        for yl in range(YL):
            got = [sum(whole_ref[(x * YH + yh) * YL + yl, q] for yh in range(YH)) for q in range(5)]
            factor = lax.rsqrt(got[4] + 1e-06)
            scale_ref[x * YL + yl] = factor
            for q in range(4):
                tiles[x, yl, q] = got[q] * factor[q:q + 1, :]
    x, yl, z, at = place_ref[0], place_ref[1], place_ref[2], place_ref[3]
    own = jnp.where(row == z // 2, scale_ref[x * YL + yl], 0.0)
    own = jnp.sum(own, axis=0, keepdims=True)
    own = jnp.where(lane == row + (z % 2) * 64 + at, own, 0.0)
    own = jnp.sum(own, axis=1, keepdims=True)
    for yl in range(YL):
        for q in range(4):
            for pair in range(2):
                low, high = tiles[2 * pair, yl, q] * own, tiles[2 * pair + 1, yl, q] * own
                even = jnp.where(lane < 64, low, pltpu.roll(high, 64, 1))
                odd = jnp.where(lane < 64, pltpu.roll(low, 64, 1), high)
                start = yl * 2048 + q * 512 + pair * 128
                out_ref[:, start:start + 128] = even
                out_ref[:, start + 256:start + 384] = odd


def finish(place, whole):
    return pl.pallas_call(
        finish_kernel,
        out_shape=jax.ShapeDtypeStruct((8, 4096), jnp.float32),
        in_specs=[SMEM, VMEM],
        out_specs=VMEM,
        scratch_shapes=[pltpu.VMEM((XS * YL, 8, 128), jnp.float32)],
        compiler_params=PARAMS,
        cost_estimate=pl.CostEstimate(flops=262144, bytes_accessed=786432, transcendentals=4096),
    )(place, whole)


def shards(grads, second_moment):
    ex, feat = lax.axis_index("ex"), lax.axis_index("feat")
    z, y_lo = ex % ZS, ex // ZS
    x, y_hi, core = feat // (YH * CS), (feat // CS) % YH, feat % CS

    scaled, copies = scale(grads, second_moment)
    swapped = lax.all_to_all(scaled.reshape(XS, 64, 256), "feat", 0, 0, axis_index_groups=X_GROUPS, tiled=True)
    piece = jnp.transpose(swapped, (1, 0, 2)).reshape(64, XS * 256)
    left = lax.all_to_all(copies, AXES, 0, 0, axis_index_groups=LEFT_GROUPS, tiled=True)
    right = ring(piece, z, 1 - 2 * core)

    mine, theirs = product(core, left, right)
    mine = mine + shift(theirs, lambda x, y, z, c: (x, y, z, c + 1))
    whole = lax.all_to_all(mine, AXES, 0, 0, axis_index_groups=XY_GROUPS, tiled=True)
    return finish(jnp.stack([x, y_lo, z, y_hi * 16 + core * 8]), whole)


def solution(mesh):
    return jax.shard_map(
        shards,
        mesh=mesh,
        in_specs=(P("ex", "feat"), P("feat")),
        out_specs=P(("ex", "feat"), None),
        check_vma=False,
    )
```

```python
import jax
import jax.numpy as jnp
from jax import lax
from jax.experimental import pallas as pl
from jax.experimental.pallas import tpu as pltpu
from jax.sharding import PartitionSpec as P

XS, YH, YL, ZS, CS = 4, 4, 2, 8, 2
YS = YH * YL
FEAT = XS * YH * CS
AXES = ("ex", "feat")
VMEM = pl.BlockSpec(memory_space=pltpu.VMEM)
SMEM = pl.BlockSpec(memory_space=pltpu.SMEM)
PARAMS = pltpu.CompilerParams(vmem_limit_bytes=32 * 1024 * 1024)


def device_at(x, y, z, c):
    return ((y % YL) * ZS + z) * FEAT + x * (YH * CS) + (y // YL) * CS + c


X_GROUPS = [[x * (YH * CS) + yh * CS + c for x in range(XS)] for yh in range(YH) for c in range(CS)]
LEFT_GROUPS = [[device_at(x, yh * YL + yl, z, c) for x in range(XS) for yl in range(YL)]
               for yh in range(YH) for z in range(ZS) for c in range(CS)]
XY_GROUPS = [[device_at(x, y, z, c) for x in range(XS) for y in range(YS)]
             for z in range(ZS) for c in range(CS)]


def shift(value, move):
    pairs = []
    for x in range(XS):
        for y in range(YS):
            for z in range(ZS):
                for c in range(CS):
                    nx, ny, nz, nc = move(x, y, z, c)
                    pairs.append((device_at(x, y, z, c), device_at(nx % XS, ny % YS, nz % ZS, nc % CS)))
    return lax.ppermute(value, AXES, pairs)


def ring(piece, at, sign, left):
    whole = lax.dynamic_update_slice(jnp.zeros((ZS,) + piece.shape, jnp.float32), piece[None], (at, 0, 0))
    ahead, behind = piece, piece
    for step in range(1, 5):
        if step == 4:
            ahead, left = lax.optimization_barrier((ahead, left))
        ahead = shift(ahead, lambda x, y, z, c: (x, y, z + (-1 if c == 0 else 1), c))
        whole = lax.dynamic_update_slice(whole, ahead[None], ((at + sign * step) % ZS, 0, 0))
        if step < 4:
            behind = shift(behind, lambda x, y, z, c: (x, y, z + (1 if c == 0 else -1), c))
            whole = lax.dynamic_update_slice(whole, behind[None], ((at - sign * step) % ZS, 0, 0))
    return whole.reshape(-1, piece.shape[1]), left


def copies_kernel(value_ref, copies_ref):
    for i in range(XS * YL):
        copies_ref[i] = value_ref[...]


def copies_of(value):
    return pl.pallas_call(
        copies_kernel,
        out_shape=jax.ShapeDtypeStruct((XS * YL, 256, 256), jnp.float32),
        in_specs=[VMEM],
        out_specs=VMEM,
        compiler_params=PARAMS,
        cost_estimate=pl.CostEstimate(flops=0, bytes_accessed=2359296, transcendentals=0),
    )(value)


def panel_kernel(blocks_ref, panel_ref):
    for x in range(XS):
        for yl in range(YL):
            panel_ref[yl * 256:(yl + 1) * 256, x * 256:(x + 1) * 256] = blocks_ref[x * YL + yl]


def panel_of(blocks):
    return pl.pallas_call(
        panel_kernel,
        out_shape=jax.ShapeDtypeStruct((YL * 256, XS * 256), jnp.float32),
        in_specs=[VMEM],
        out_specs=VMEM,
        compiler_params=PARAMS,
        cost_estimate=pl.CostEstimate(flops=0, bytes_accessed=4194304, transcendentals=0),
    )(blocks)


def finish_kernel(place_ref, whole_ref, out_ref, scale_ref):
    row = lax.broadcasted_iota(jnp.int32, (8, 128), 0)
    lane = lax.broadcasted_iota(jnp.int32, (8, 128), 1)
    tiles = {}
    for x in range(XS):
        for yl in range(YL):
            got = [sum(whole_ref[(x * YH + yh) * YL + yl, q] for yh in range(YH)) for q in range(5)]
            factor = lax.rsqrt(got[4] + 1e-06)
            scale_ref[x * YL + yl] = factor
            for q in range(4):
                tiles[x, yl, q] = got[q] * factor[q:q + 1, :]
    x, yl, z, at = place_ref[0], place_ref[1], place_ref[2], place_ref[3]
    own = jnp.where(row == z // 2, scale_ref[x * YL + yl], 0.0)
    own = jnp.sum(own, axis=0, keepdims=True)
    own = jnp.where(lane == row + (z % 2) * 64 + at, own, 0.0)
    own = jnp.sum(own, axis=1, keepdims=True)
    for yl in range(YL):
        for q in range(4):
            for pair in range(2):
                low, high = tiles[2 * pair, yl, q] * own, tiles[2 * pair + 1, yl, q] * own
                even = jnp.where(lane < 64, low, pltpu.roll(high, 64, 1))
                odd = jnp.where(lane < 64, pltpu.roll(low, 64, 1), high)
                start = yl * 2048 + q * 512 + pair * 128
                out_ref[:, start:start + 128] = even
                out_ref[:, start + 256:start + 384] = odd


def finish(place, whole):
    return pl.pallas_call(
        finish_kernel,
        out_shape=jax.ShapeDtypeStruct((8, 4096), jnp.float32),
        in_specs=[SMEM, VMEM],
        out_specs=VMEM,
        scratch_shapes=[pltpu.VMEM((XS * YL, 8, 128), jnp.float32)],
        compiler_params=PARAMS,
        cost_estimate=pl.CostEstimate(flops=262144, bytes_accessed=786432, transcendentals=4096),
    )(place, whole)


def shards(grads, second_moment):
    ex, feat = lax.axis_index("ex"), lax.axis_index("feat")
    z, y_lo = ex % ZS, ex // ZS
    x, y_hi, core = feat // (YH * CS), (feat // CS) % YH, feat % CS

    scaled = grads * (1.0 / (jnp.sqrt(second_moment) + 1e-08))[None, :]
    swapped = lax.all_to_all(scaled.reshape(XS, 64, 256), "feat", 0, 0, axis_index_groups=X_GROUPS, tiled=True)
    piece = jnp.transpose(swapped, (1, 0, 2)).reshape(64, XS * 256)
    scaled, piece = lax.optimization_barrier((scaled, piece))
    blocks = lax.all_to_all(copies_of(scaled), AXES, 0, 0, axis_index_groups=LEFT_GROUPS, tiled=True)
    right, left = ring(piece, z, 1 - 2 * core, panel_of(blocks))

    part = lax.dot_general(left, right, (((1,), (1,)), ((), ())), precision=lax.Precision.HIGH,
                           preferred_element_type=jnp.float32)
    sums = jnp.sum(right * right, axis=1)
    part = jnp.transpose(part.reshape(YL, XS, YH, CS, 8, 4, 128), (3, 1, 2, 0, 5, 4, 6)).reshape(CS, XS * YS, 4, 8, 128)
    sums = jnp.broadcast_to(jnp.pad(sums.reshape(4, 128), ((0, 4), (0, 0))), (CS, XS * YS, 1, 8, 128))
    part = jnp.concatenate([part, sums], axis=2)
    take = lambda i: lax.dynamic_index_in_dim(part, i, 0, keepdims=False)
    mine = take(core) + shift(take(1 - core), lambda x, y, z, c: (x, y, z, c + 1))
    whole = lax.all_to_all(mine, AXES, 0, 0, axis_index_groups=XY_GROUPS, tiled=True)
    return finish(jnp.stack([x, y_lo, z, y_hi * 16 + core * 8]), whole)


def solution(mesh):
    return jax.shard_map(
        shards,
        mesh=mesh,
        in_specs=(P("ex", "feat"), P("feat")),
        out_specs=P(("ex", "feat"), None),
        check_vma=False,
    )
```

```python
import jax
import jax.numpy as jnp
from jax import lax
from jax.experimental import pallas as pl
from jax.experimental.pallas import tpu as pltpu
from jax.sharding import PartitionSpec as P

XS, YH, YL, ZS, CS = 4, 4, 2, 8, 2
YS = YH * YL
FEAT = XS * YH * CS
AXES = ("ex", "feat")
VMEM = pl.BlockSpec(memory_space=pltpu.VMEM)
SMEM = pl.BlockSpec(memory_space=pltpu.SMEM)
PARAMS = pltpu.CompilerParams(vmem_limit_bytes=32 * 1024 * 1024)


def device_at(x, y, z, c):
    return ((y % YL) * ZS + z) * FEAT + x * (YH * CS) + (y // YL) * CS + c


X_GROUPS = [[x * (YH * CS) + yh * CS + c for x in range(XS)] for yh in range(YH) for c in range(CS)]
LEFT_GROUPS = [[device_at(x, yh * YL + yl, z, c) for x in range(XS) for yl in range(YL)]
               for yh in range(YH) for z in range(ZS) for c in range(CS)]
XY_GROUPS = [[device_at(x, y, z, c) for x in range(XS) for y in range(YS)]
             for z in range(ZS) for c in range(CS)]


def shift(value, move):
    pairs = []
    for x in range(XS):
        for y in range(YS):
            for z in range(ZS):
                for c in range(CS):
                    nx, ny, nz, nc = move(x, y, z, c)
                    pairs.append((device_at(x, y, z, c), device_at(nx % XS, ny % YS, nz % ZS, nc % CS)))
    return lax.ppermute(value, AXES, pairs)


def ring(piece, at, sign):
    whole = lax.dynamic_update_slice(jnp.zeros((ZS,) + piece.shape, jnp.float32), piece[None], (at, 0, 0))
    ahead, behind = piece, piece
    for step in range(1, 5):
        ahead = shift(ahead, lambda x, y, z, c: (x, y, z + (-1 if c == 0 else 1), c))
        first = ahead if step == 1 else first
        whole = lax.dynamic_update_slice(whole, ahead[None], ((at + sign * step) % ZS, 0, 0))
        if step < 4:
            behind = shift(behind, lambda x, y, z, c: (x, y, z + (1 if c == 0 else -1), c))
            whole = lax.dynamic_update_slice(whole, behind[None], ((at - sign * step) % ZS, 0, 0))
    return whole.reshape(-1, piece.shape[1]), first


def copies_kernel(value_ref, copies_ref):
    for i in range(XS * YL):
        copies_ref[i] = value_ref[...]


def copies_of(value):
    return pl.pallas_call(
        copies_kernel,
        out_shape=jax.ShapeDtypeStruct((XS * YL, 256, 256), jnp.float32),
        in_specs=[VMEM],
        out_specs=VMEM,
        compiler_params=PARAMS,
        cost_estimate=pl.CostEstimate(flops=0, bytes_accessed=2359296, transcendentals=0),
    )(value)


def halves(value):
    high = value.astype(jnp.bfloat16)
    return high, (value - high.astype(jnp.float32)).astype(jnp.bfloat16)


def dot_t(left, right):
    return lax.dot_general(left, right, (((1,), (1,)), ((), ())), preferred_element_type=jnp.float32)


def product_kernel(core_ref, left_ref, right_ref, mine_ref, theirs_ref, total_ref):
    ones = jnp.ones((8, 256), jnp.bfloat16)
    sums = jnp.zeros((8, 512), jnp.float32)
    for x in range(XS):
        block = right_ref[:, x * 256:(x + 1) * 256]
        right_high, right_low = halves(block)
        square_high, square_low = halves(block * block)
        sums = sums + dot_t(ones, square_high) + dot_t(ones, square_low)
        for yl in range(YL):
            left_high, left_low = halves(left_ref[x * YL + yl])
            part = dot_t(left_high, right_high) + dot_t(left_high, right_low) + dot_t(left_low, right_high)
            if x == 0:
                total_ref[yl] = part
            else:
                total_ref[yl] += part
    row = lax.broadcasted_iota(jnp.int32, (8, 128), 0)
    tile = jnp.zeros((8, 128), jnp.float32)
    for q in range(4):
        tile = jnp.where(row == q, sums[:, q * 128:(q + 1) * 128], tile)

    def write(refs):
        for x in range(XS):
            for yh in range(YH):
                for yl in range(YL):
                    to = (x * YH + yh) * YL + yl
                    for c in range(CS):
                        at = x * 64 + yh * 16 + c * 8
                        for q in range(4):
                            refs[c][to, q] = total_ref[yl, at:at + 8, q * 128:(q + 1) * 128]
                        refs[c][to, 4] = tile

    @pl.when(core_ref[0] == 0)
    def _():
        write((mine_ref, theirs_ref))

    @pl.when(core_ref[0] == 1)
    def _():
        write((theirs_ref, mine_ref))


def product(core, left, right):
    message = jax.ShapeDtypeStruct((XS * YS, 5, 8, 128), jnp.float32)
    return pl.pallas_call(
        product_kernel,
        out_shape=(message, message),
        in_specs=[SMEM, VMEM, VMEM],
        out_specs=(VMEM, VMEM),
        scratch_shapes=[pltpu.VMEM((YL, 256, 512), jnp.float32)],
        compiler_params=PARAMS,
        cost_estimate=pl.CostEstimate(flops=3 * 2 * 512 * 512 * 1024, bytes_accessed=5505024, transcendentals=0),
    )(core.reshape(1), left, right)


def finish_kernel(place_ref, whole_ref, out_ref, scale_ref):
    row = lax.broadcasted_iota(jnp.int32, (8, 128), 0)
    lane = lax.broadcasted_iota(jnp.int32, (8, 128), 1)
    tiles = {}
    for x in range(XS):
        for yl in range(YL):
            got = [sum(whole_ref[(x * YH + yh) * YL + yl, q] for yh in range(YH)) for q in range(5)]
            factor = lax.rsqrt(got[4] + 1e-06)
            scale_ref[x * YL + yl] = factor
            for q in range(4):
                tiles[x, yl, q] = got[q] * factor[q:q + 1, :]
    x, yl, z, at = place_ref[0], place_ref[1], place_ref[2], place_ref[3]
    own = jnp.where(row == z // 2, scale_ref[x * YL + yl], 0.0)
    own = jnp.sum(own, axis=0, keepdims=True)
    own = jnp.where(lane == row + (z % 2) * 64 + at, own, 0.0)
    own = jnp.sum(own, axis=1, keepdims=True)
    for yl in range(YL):
        for q in range(4):
            for pair in range(2):
                low, high = tiles[2 * pair, yl, q] * own, tiles[2 * pair + 1, yl, q] * own
                even = jnp.where(lane < 64, low, pltpu.roll(high, 64, 1))
                odd = jnp.where(lane < 64, pltpu.roll(low, 64, 1), high)
                start = yl * 2048 + q * 512 + pair * 128
                out_ref[:, start:start + 128] = even
                out_ref[:, start + 256:start + 384] = odd


def finish(place, whole):
    return pl.pallas_call(
        finish_kernel,
        out_shape=jax.ShapeDtypeStruct((8, 4096), jnp.float32),
        in_specs=[SMEM, VMEM],
        out_specs=VMEM,
        scratch_shapes=[pltpu.VMEM((XS * YL, 8, 128), jnp.float32)],
        compiler_params=PARAMS,
        cost_estimate=pl.CostEstimate(flops=262144, bytes_accessed=786432, transcendentals=4096),
    )(place, whole)


def shards(grads, second_moment):
    ex, feat = lax.axis_index("ex"), lax.axis_index("feat")
    z, y_lo = ex % ZS, ex // ZS
    x, y_hi, core = feat // (YH * CS), (feat // CS) % YH, feat % CS

    scaled = grads * (1.0 / (jnp.sqrt(second_moment) + 1e-08))[None, :]
    copies = copies_of(scaled)
    swapped = lax.all_to_all(scaled.reshape(XS, 64, 256), "feat", 0, 0, axis_index_groups=X_GROUPS, tiled=True)
    piece = jnp.transpose(swapped, (1, 0, 2)).reshape(64, XS * 256)
    right, first = ring(piece, z, 1 - 2 * core)
    copies, _ = lax.optimization_barrier((copies, first))
    left = lax.all_to_all(copies, AXES, 0, 0, axis_index_groups=LEFT_GROUPS, tiled=True)

    mine, theirs = product(core, left, right)
    mine = mine + shift(theirs, lambda x, y, z, c: (x, y, z, c + 1))
    whole = lax.all_to_all(mine, AXES, 0, 0, axis_index_groups=XY_GROUPS, tiled=True)
    return finish(jnp.stack([x, y_lo, z, y_hi * 16 + core * 8]), whole)


def solution(mesh):
    return jax.shard_map(
        shards,
        mesh=mesh,
        in_specs=(P("ex", "feat"), P("feat")),
        out_specs=P(("ex", "feat"), None),
        check_vma=False,
    )
```

```python
import jax
import jax.numpy as jnp
from jax import lax
from jax.experimental import pallas as pl
from jax.experimental.pallas import tpu as pltpu
from jax.sharding import PartitionSpec as P

XS, YH, YL, ZS, CS = 4, 4, 2, 8, 2
YS = YH * YL
FEAT = XS * YH * CS
AXES = ("ex", "feat")
VMEM = pl.BlockSpec(memory_space=pltpu.VMEM)
SMEM = pl.BlockSpec(memory_space=pltpu.SMEM)
PARAMS = pltpu.CompilerParams(vmem_limit_bytes=32 * 1024 * 1024)


def device_at(x, y, z, c):
    return ((y % YL) * ZS + z) * FEAT + x * (YH * CS) + (y // YL) * CS + c


X_GROUPS = [[x * (YH * CS) + yh * CS + c for x in range(XS)] for yh in range(YH) for c in range(CS)]
LEFT_GROUPS = [[device_at(x, yh * YL + yl, z, c) for x in range(XS) for yl in range(YL)]
               for yh in range(YH) for z in range(ZS) for c in range(CS)]
XY_GROUPS = [[device_at(x, y, z, c) for x in range(XS) for y in range(YS)]
             for z in range(ZS) for c in range(CS)]


def shift(value, move):
    pairs = []
    for x in range(XS):
        for y in range(YS):
            for z in range(ZS):
                for c in range(CS):
                    nx, ny, nz, nc = move(x, y, z, c)
                    pairs.append((device_at(x, y, z, c), device_at(nx % XS, ny % YS, nz % ZS, nc % CS)))
    return lax.ppermute(value, AXES, pairs)


def ring(piece, at, sign):
    whole = lax.dynamic_update_slice(jnp.zeros((ZS,) + piece.shape, jnp.float32), piece[None], (at, 0, 0))
    ahead, behind = piece, piece
    for step in range(1, 5):
        ahead = shift(ahead, lambda x, y, z, c: (x, y, z + (-1 if c == 0 else 1), c))
        whole = lax.dynamic_update_slice(whole, ahead[None], ((at + sign * step) % ZS, 0, 0))
        if step < 4:
            behind = shift(behind, lambda x, y, z, c: (x, y, z + (1 if c == 0 else -1), c))
            first = behind if step == 1 else first
            whole = lax.dynamic_update_slice(whole, behind[None], ((at - sign * step) % ZS, 0, 0))
    return whole.reshape(-1, piece.shape[1]), first


def copies_kernel(value_ref, copies_ref):
    for i in range(XS * YL):
        copies_ref[i] = value_ref[...]


def copies_of(value):
    return pl.pallas_call(
        copies_kernel,
        out_shape=jax.ShapeDtypeStruct((XS * YL, 256, 256), jnp.float32),
        in_specs=[VMEM],
        out_specs=VMEM,
        compiler_params=PARAMS,
        cost_estimate=pl.CostEstimate(flops=0, bytes_accessed=2359296, transcendentals=0),
    )(value)


def halves(value):
    high = value.astype(jnp.bfloat16)
    return high, (value - high.astype(jnp.float32)).astype(jnp.bfloat16)


def dot_t(left, right):
    return lax.dot_general(left, right, (((1,), (1,)), ((), ())), preferred_element_type=jnp.float32)


def product_kernel(core_ref, left_ref, right_ref, mine_ref, theirs_ref, total_ref):
    ones = jnp.ones((8, 256), jnp.bfloat16)
    sums = jnp.zeros((8, 512), jnp.float32)
    for x in range(XS):
        block = right_ref[:, x * 256:(x + 1) * 256]
        right_high, right_low = halves(block)
        square_high, square_low = halves(block * block)
        sums = sums + dot_t(ones, square_high) + dot_t(ones, square_low)
        for yl in range(YL):
            left_high, left_low = halves(left_ref[x * YL + yl])
            part = dot_t(left_high, right_high) + dot_t(left_high, right_low) + dot_t(left_low, right_high)
            if x == 0:
                total_ref[yl] = part
            else:
                total_ref[yl] += part
    row = lax.broadcasted_iota(jnp.int32, (8, 128), 0)
    tile = jnp.zeros((8, 128), jnp.float32)
    for q in range(4):
        tile = jnp.where(row == q, sums[:, q * 128:(q + 1) * 128], tile)

    def write(refs):
        for x in range(XS):
            for yh in range(YH):
                for yl in range(YL):
                    to = (x * YH + yh) * YL + yl
                    for c in range(CS):
                        at = x * 64 + yh * 16 + c * 8
                        for q in range(4):
                            refs[c][to, q] = total_ref[yl, at:at + 8, q * 128:(q + 1) * 128]
                        refs[c][to, 4] = tile

    @pl.when(core_ref[0] == 0)
    def _():
        write((mine_ref, theirs_ref))

    @pl.when(core_ref[0] == 1)
    def _():
        write((theirs_ref, mine_ref))


def product(core, left, right):
    message = jax.ShapeDtypeStruct((XS * YS, 5, 8, 128), jnp.float32)
    return pl.pallas_call(
        product_kernel,
        out_shape=(message, message),
        in_specs=[SMEM, VMEM, VMEM],
        out_specs=(VMEM, VMEM),
        scratch_shapes=[pltpu.VMEM((YL, 256, 512), jnp.float32)],
        compiler_params=PARAMS,
        cost_estimate=pl.CostEstimate(flops=3 * 2 * 512 * 512 * 1024, bytes_accessed=5505024, transcendentals=0),
    )(core.reshape(1), left, right)


def finish_kernel(place_ref, whole_ref, out_ref, scale_ref):
    row = lax.broadcasted_iota(jnp.int32, (8, 128), 0)
    lane = lax.broadcasted_iota(jnp.int32, (8, 128), 1)
    tiles = {}
    for x in range(XS):
        for yl in range(YL):
            got = [sum(whole_ref[(x * YH + yh) * YL + yl, q] for yh in range(YH)) for q in range(5)]
            factor = lax.rsqrt(got[4] + 1e-06)
            scale_ref[x * YL + yl] = factor
            for q in range(4):
                tiles[x, yl, q] = got[q] * factor[q:q + 1, :]
    x, yl, z, at = place_ref[0], place_ref[1], place_ref[2], place_ref[3]
    own = jnp.where(row == z // 2, scale_ref[x * YL + yl], 0.0)
    own = jnp.sum(own, axis=0, keepdims=True)
    own = jnp.where(lane == row + (z % 2) * 64 + at, own, 0.0)
    own = jnp.sum(own, axis=1, keepdims=True)
    for yl in range(YL):
        for q in range(4):
            for pair in range(2):
                low, high = tiles[2 * pair, yl, q] * own, tiles[2 * pair + 1, yl, q] * own
                even = jnp.where(lane < 64, low, pltpu.roll(high, 64, 1))
                odd = jnp.where(lane < 64, pltpu.roll(low, 64, 1), high)
                start = yl * 2048 + q * 512 + pair * 128
                out_ref[:, start:start + 128] = even
                out_ref[:, start + 256:start + 384] = odd


def finish(place, whole):
    return pl.pallas_call(
        finish_kernel,
        out_shape=jax.ShapeDtypeStruct((8, 4096), jnp.float32),
        in_specs=[SMEM, VMEM],
        out_specs=VMEM,
        scratch_shapes=[pltpu.VMEM((XS * YL, 8, 128), jnp.float32)],
        compiler_params=PARAMS,
        cost_estimate=pl.CostEstimate(flops=262144, bytes_accessed=786432, transcendentals=4096),
    )(place, whole)


def shards(grads, second_moment):
    ex, feat = lax.axis_index("ex"), lax.axis_index("feat")
    z, y_lo = ex % ZS, ex // ZS
    x, y_hi, core = feat // (YH * CS), (feat // CS) % YH, feat % CS

    scaled = grads * (1.0 / (jnp.sqrt(second_moment) + 1e-08))[None, :]
    copies = copies_of(scaled)
    swapped = lax.all_to_all(scaled.reshape(XS, 64, 256), "feat", 0, 0, axis_index_groups=X_GROUPS, tiled=True)
    piece = jnp.transpose(swapped, (1, 0, 2)).reshape(64, XS * 256)
    right, first = ring(piece, z, 1 - 2 * core)
    copies, _ = lax.optimization_barrier((copies, first))
    left = lax.all_to_all(copies, AXES, 0, 0, axis_index_groups=LEFT_GROUPS, tiled=True)

    mine, theirs = product(core, left, right)
    mine = mine + shift(theirs, lambda x, y, z, c: (x, y, z, c + 1))
    whole = lax.all_to_all(mine, AXES, 0, 0, axis_index_groups=XY_GROUPS, tiled=True)
    return finish(jnp.stack([x, y_lo, z, y_hi * 16 + core * 8]), whole)


def solution(mesh):
    return jax.shard_map(
        shards,
        mesh=mesh,
        in_specs=(P("ex", "feat"), P("feat")),
        out_specs=P(("ex", "feat"), None),
        check_vma=False,
    )
```

```python
import functools

import jax
import jax.numpy as jnp
from jax import lax
from jax.experimental import pallas as pl
from jax.experimental.pallas import tpu as pltpu
from jax.sharding import PartitionSpec as P

XS, YH, YL, ZS, CS = 4, 4, 2, 8, 2
YS = YH * YL
FEAT = XS * YH * CS
AXES = ("ex", "feat")
VMEM = pl.BlockSpec(memory_space=pltpu.VMEM)
SMEM = pl.BlockSpec(memory_space=pltpu.SMEM)
PARAMS = pltpu.CompilerParams(vmem_limit_bytes=32 * 1024 * 1024)


def device_at(x, y, z, c):
    return ((y % YL) * ZS + z) * FEAT + x * (YH * CS) + (y // YL) * CS + c


X_GROUPS = [[x * (YH * CS) + yh * CS + c for x in range(XS)] for yh in range(YH) for c in range(CS)]
LEFT_GROUPS = [[device_at(x, yh * YL + yl, z, c) for x in range(XS) for yl in range(YL)]
               for yh in range(YH) for z in range(ZS) for c in range(CS)]
XY_GROUPS = [[device_at(x, y, z, c) for x in range(XS) for y in range(YS)]
             for z in range(ZS) for c in range(CS)]


def shift(value, move):
    pairs = []
    for x in range(XS):
        for y in range(YS):
            for z in range(ZS):
                for c in range(CS):
                    nx, ny, nz, nc = move(x, y, z, c)
                    pairs.append((device_at(x, y, z, c), device_at(nx % XS, ny % YS, nz % ZS, nc % CS)))
    return lax.ppermute(value, AXES, pairs)


def ring(piece, at, sign):
    whole = lax.dynamic_update_slice(jnp.zeros((ZS,) + piece.shape, jnp.float32), piece[None], (at, 0, 0))
    ahead, behind = piece, piece
    for step in range(1, 5):
        ahead = shift(ahead, lambda x, y, z, c: (x, y, z + (-1 if c == 0 else 1), c))
        whole = lax.dynamic_update_slice(whole, ahead[None], ((at + sign * step) % ZS, 0, 0))
        if step < 4:
            behind = shift(behind, lambda x, y, z, c: (x, y, z + (1 if c == 0 else -1), c))
            whole = lax.dynamic_update_slice(whole, behind[None], ((at - sign * step) % ZS, 0, 0))
    return whole.reshape(-1, piece.shape[1])


def scale_kernel(grads_ref, moment_ref, scaled_ref, copies_ref):
    scaled = grads_ref[...] * (1.0 / (jnp.sqrt(moment_ref[...]) + 1e-08))
    scaled_ref[...] = scaled
    for i in range(XS * YL):
        copies_ref[i] = scaled


def scale(grads, second_moment):
    return pl.pallas_call(
        scale_kernel,
        out_shape=(jax.ShapeDtypeStruct((256, 256), jnp.float32),
                   jax.ShapeDtypeStruct((XS * YL, 256, 256), jnp.float32)),
        in_specs=[VMEM, VMEM],
        out_specs=(VMEM, VMEM),
        compiler_params=PARAMS,
        cost_estimate=pl.CostEstimate(flops=65536, bytes_accessed=2621440, transcendentals=256),
    )(grads, second_moment.reshape(1, 256))


def halves(value):
    high = value.astype(jnp.bfloat16)
    return high, (value - high.astype(jnp.float32)).astype(jnp.bfloat16)


def dot_t(left, right):
    return lax.dot_general(left, right, (((1,), (1,)), ((), ())), preferred_element_type=jnp.float32)


def half_kernel(first, core_ref, left_ref, right_ref, *refs):
    message_ref, tile_ref, total_ref = (refs[0], refs[1], refs[2]) if first else (refs[1], refs[0], refs[2])
    core = core_ref[0]
    ones = jnp.ones((8, 256), jnp.bfloat16)
    sums = jnp.zeros((8, 512), jnp.float32)
    for x in range(XS):
        block = right_ref[:, x * 256:(x + 1) * 256]
        right_high, right_low = halves(block)
        if first:
            square_high, square_low = halves(block * block)
            sums = sums + dot_t(ones, square_high) + dot_t(ones, square_low)
        rows = [left_ref[x * YL + yl, pl.ds(pl.multiple_of(i * 16 + core * 8, 8), 8), :]
                for yl in range(YL) for i in range(XS * YH)]
        left_high, left_low = halves(jnp.concatenate(rows, axis=0))
        part = dot_t(left_high, right_high) + dot_t(left_high, right_low) + dot_t(left_low, right_high)
        if x == 0:
            total_ref[...] = part
        else:
            total_ref[...] += part
    if first:
        row = lax.broadcasted_iota(jnp.int32, (4, 128), 0)
        tile = jnp.zeros((4, 128), jnp.float32)
        for q in range(4):
            tile = jnp.where(row == q, sums[:4, q * 128:(q + 1) * 128], tile)
        tile_ref[...] = tile
    else:
        tile = tile_ref[...]
    for yl in range(YL):
        for i in range(XS * YH):
            to = i * YL + yl
            for q in range(4):
                for half in range(2):
                    top = (yl * XS * YH + i) * 8 + 4 * half
                    message_ref[to, 2 * q + half] = total_ref[top:top + 4, q * 128:(q + 1) * 128]
            message_ref[to, 8] = tile


def half_product(core, left, right, tile=None):
    first = tile is None
    message = jax.ShapeDtypeStruct((XS * YS, 9, 4, 128), jnp.float32)
    sums = jax.ShapeDtypeStruct((4, 128), jnp.float32)
    return pl.pallas_call(
        functools.partial(half_kernel, first),
        out_shape=(message, sums) if first else message,
        in_specs=[SMEM] + [VMEM] * (2 if first else 3),
        out_specs=(VMEM, VMEM) if first else VMEM,
        scratch_shapes=[pltpu.VMEM((256, 512), jnp.float32)],
        compiler_params=PARAMS,
        cost_estimate=pl.CostEstimate(flops=3 * 2 * 256 * 512 * 1024, bytes_accessed=4784128, transcendentals=0),
    )(core.reshape(1), left, right, *(() if first else (tile,)))


def finish_kernel(place_ref, whole_ref, out_ref, scale_ref):
    row = lax.broadcasted_iota(jnp.int32, (8, 128), 0)
    part = lax.broadcasted_iota(jnp.int32, (4, 128), 0)
    lane = lax.broadcasted_iota(jnp.int32, (8, 128), 1)
    tiles = {}
    for x in range(XS):
        for yl in range(YL):
            got = [sum(whole_ref[(x * YH + yh) * YL + yl, q] for yh in range(YH)) for q in range(9)]
            factor = lax.rsqrt(got[8] + 1e-06)
            scale_ref[x * YL + yl] = factor
            for q in range(4):
                tile = jnp.concatenate([got[2 * q], got[2 * q + 1]], axis=0)
                tiles[x, yl, q] = tile * factor[q:q + 1, :]
    x, yl, z, at = place_ref[0], place_ref[1], place_ref[2], place_ref[3]
    own = jnp.where(part == z // 2, scale_ref[x * YL + yl], 0.0)
    own = jnp.sum(own, axis=0, keepdims=True)
    own = jnp.where(lane == row + (z % 2) * 64 + at, own, 0.0)
    own = jnp.sum(own, axis=1, keepdims=True)
    for yl in range(YL):
        for q in range(4):
            for pair in range(2):
                low, high = tiles[2 * pair, yl, q] * own, tiles[2 * pair + 1, yl, q] * own
                even = jnp.where(lane < 64, low, pltpu.roll(high, 64, 1))
                odd = jnp.where(lane < 64, pltpu.roll(low, 64, 1), high)
                start = yl * 2048 + q * 512 + pair * 128
                out_ref[:, start:start + 128] = even
                out_ref[:, start + 256:start + 384] = odd


def finish(place, whole):
    return pl.pallas_call(
        finish_kernel,
        out_shape=jax.ShapeDtypeStruct((8, 4096), jnp.float32),
        in_specs=[SMEM, VMEM],
        out_specs=VMEM,
        scratch_shapes=[pltpu.VMEM((XS * YL, 4, 128), jnp.float32)],
        compiler_params=PARAMS,
        cost_estimate=pl.CostEstimate(flops=262144, bytes_accessed=786432, transcendentals=4096),
    )(place, whole)


def shards(grads, second_moment):
    ex, feat = lax.axis_index("ex"), lax.axis_index("feat")
    z, y_lo = ex % ZS, ex // ZS
    x, y_hi, core = feat // (YH * CS), (feat // CS) % YH, feat % CS

    scaled, copies = scale(grads, second_moment)
    swapped = lax.all_to_all(scaled.reshape(XS, 64, 256), "feat", 0, 0, axis_index_groups=X_GROUPS, tiled=True)
    piece = jnp.transpose(swapped, (1, 0, 2)).reshape(64, XS * 256)
    left = lax.all_to_all(copies, AXES, 0, 0, axis_index_groups=LEFT_GROUPS, tiled=True)
    right = ring(piece, z, 1 - 2 * core)

    theirs, tile = half_product(1 - core, left, right)
    theirs = shift(theirs, lambda x, y, z, c: (x, y, z, c + 1))
    mine = half_product(core, left, right, tile) + theirs
    whole = lax.all_to_all(mine, AXES, 0, 0, axis_index_groups=XY_GROUPS, tiled=True)
    return finish(jnp.stack([x, y_lo, z, y_hi * 16 + core * 8]), whole)


def solution(mesh):
    return jax.shard_map(
        shards,
        mesh=mesh,
        in_specs=(P("ex", "feat"), P("feat")),
        out_specs=P(("ex", "feat"), None),
        check_vma=False,
    )
```

```python
import functools

import jax
import jax.numpy as jnp
from jax import lax
from jax.experimental import pallas as pl
from jax.experimental.pallas import tpu as pltpu
from jax.sharding import PartitionSpec as P

XS, YH, YL, ZS, CS = 4, 4, 2, 8, 2
YS = YH * YL
FEAT = XS * YH * CS
AXES = ("ex", "feat")
VMEM = pl.BlockSpec(memory_space=pltpu.VMEM)
SMEM = pl.BlockSpec(memory_space=pltpu.SMEM)
PARAMS = pltpu.CompilerParams(vmem_limit_bytes=32 * 1024 * 1024)


def device_at(x, y, z, c):
    return ((y % YL) * ZS + z) * FEAT + x * (YH * CS) + (y // YL) * CS + c


X_GROUPS = [[x * (YH * CS) + yh * CS + c for x in range(XS)] for yh in range(YH) for c in range(CS)]
LEFT_GROUPS = [[device_at(x, yh * YL + yl, z, c) for x in range(XS) for yl in range(YL)]
               for yh in range(YH) for z in range(ZS) for c in range(CS)]
XY_GROUPS = [[device_at(x, y, z, c) for x in range(XS) for y in range(YS)]
             for z in range(ZS) for c in range(CS)]


def shift(value, move):
    pairs = []
    for x in range(XS):
        for y in range(YS):
            for z in range(ZS):
                for c in range(CS):
                    nx, ny, nz, nc = move(x, y, z, c)
                    pairs.append((device_at(x, y, z, c), device_at(nx % XS, ny % YS, nz % ZS, nc % CS)))
    return lax.ppermute(value, AXES, pairs)


def ring(piece, at, sign):
    whole = lax.dynamic_update_slice(jnp.zeros((ZS,) + piece.shape, jnp.float32), piece[None], (at, 0, 0))
    ahead, behind = piece, piece
    for step in range(1, 5):
        ahead = shift(ahead, lambda x, y, z, c: (x, y, z + (-1 if c == 0 else 1), c))
        whole = lax.dynamic_update_slice(whole, ahead[None], ((at + sign * step) % ZS, 0, 0))
        if step < 4:
            behind = shift(behind, lambda x, y, z, c: (x, y, z + (1 if c == 0 else -1), c))
            whole = lax.dynamic_update_slice(whole, behind[None], ((at - sign * step) % ZS, 0, 0))
    return whole.reshape(-1, piece.shape[1])


def scale_kernel(grads_ref, moment_ref, scaled_ref, copies_ref):
    scaled = grads_ref[...] * (1.0 / (jnp.sqrt(moment_ref[...]) + 1e-08))
    scaled_ref[...] = scaled
    for i in range(XS * YL):
        copies_ref[i] = scaled


def scale(grads, second_moment):
    return pl.pallas_call(
        scale_kernel,
        out_shape=(jax.ShapeDtypeStruct((256, 256), jnp.float32),
                   jax.ShapeDtypeStruct((XS * YL, 256, 256), jnp.float32)),
        in_specs=[VMEM, VMEM],
        out_specs=(VMEM, VMEM),
        compiler_params=PARAMS,
        cost_estimate=pl.CostEstimate(flops=65536, bytes_accessed=2621440, transcendentals=256),
    )(grads, second_moment.reshape(1, 256))


def halves(value):
    high = value.astype(jnp.bfloat16)
    return high, (value - high.astype(jnp.float32)).astype(jnp.bfloat16)


def dot_t(left, right):
    return lax.dot_general(left, right, (((1,), (1,)), ((), ())), preferred_element_type=jnp.float32)


def half_kernel(first, core_ref, left_ref, right_ref, *refs):
    message_ref, tile_ref, total_ref = (refs[0], refs[1], refs[3]) if first else (refs[1], refs[0], refs[2])
    core = core_ref[0]
    ones = jnp.ones((8, 256), jnp.bfloat16)
    sums = jnp.zeros((8, 512), jnp.float32)
    for x in range(XS):
        block = right_ref[:, x * 256:(x + 1) * 256]
        right_high, right_low = halves(block)
        if first:
            square_high, square_low = halves(block * block)
            sums = sums + dot_t(ones, square_high) + dot_t(ones, square_low)
        rows = [left_ref[x * YL + yl, pl.ds(pl.multiple_of(i * 16 + core * 8, 8), 8), :]
                for yl in range(YL) for i in range(XS * YH)]
        left_high, left_low = halves(jnp.concatenate(rows, axis=0))
        part = dot_t(left_high, right_high) + dot_t(left_high, right_low) + dot_t(left_low, right_high)
        if x == 0:
            total_ref[...] = part
        else:
            total_ref[...] += part
    if first:
        row = lax.broadcasted_iota(jnp.int32, (4, 128), 0)
        tile = jnp.zeros((4, 128), jnp.float32)
        for q in range(4):
            tile = jnp.where(row == q, sums[:4, q * 128:(q + 1) * 128], tile)
        tile_ref[...] = tile
    else:
        tile = tile_ref[...]
    for yl in range(YL):
        for i in range(XS * YH):
            to = i * YL + yl
            for q in range(4):
                for half in range(2):
                    top = (yl * XS * YH + i) * 8 + 4 * half
                    message_ref[to, 2 * q + half] = total_ref[top:top + 4, q * 128:(q + 1) * 128]
            message_ref[to, 8] = tile


def half_product(core, left, right, tile=None):
    first = tile is None
    message = jax.ShapeDtypeStruct((XS * YS, 9, 4, 128), jnp.float32)
    sums = jax.ShapeDtypeStruct((4, 128), jnp.float32)
    same = jax.ShapeDtypeStruct(right.shape, jnp.float32)
    return pl.pallas_call(
        functools.partial(half_kernel, first),
        out_shape=(message, sums, same) if first else message,
        in_specs=[SMEM] + [VMEM] * (2 if first else 3),
        out_specs=(VMEM, VMEM, VMEM) if first else VMEM,
        input_output_aliases={2: 2} if first else {},
        scratch_shapes=[pltpu.VMEM((256, 512), jnp.float32)],
        compiler_params=PARAMS,
        cost_estimate=pl.CostEstimate(flops=3 * 2 * 256 * 512 * 1024, bytes_accessed=4784128, transcendentals=0),
    )(core.reshape(1), left, right, *(() if first else (tile,)))


def finish_kernel(place_ref, whole_ref, out_ref, scale_ref):
    row = lax.broadcasted_iota(jnp.int32, (8, 128), 0)
    part = lax.broadcasted_iota(jnp.int32, (4, 128), 0)
    lane = lax.broadcasted_iota(jnp.int32, (8, 128), 1)
    tiles = {}
    for x in range(XS):
        for yl in range(YL):
            got = [sum(whole_ref[(x * YH + yh) * YL + yl, q] for yh in range(YH)) for q in range(9)]
            factor = lax.rsqrt(got[8] + 1e-06)
            scale_ref[x * YL + yl] = factor
            for q in range(4):
                tile = jnp.concatenate([got[2 * q], got[2 * q + 1]], axis=0)
                tiles[x, yl, q] = tile * factor[q:q + 1, :]
    x, yl, z, at = place_ref[0], place_ref[1], place_ref[2], place_ref[3]
    own = jnp.where(part == z // 2, scale_ref[x * YL + yl], 0.0)
    own = jnp.sum(own, axis=0, keepdims=True)
    own = jnp.where(lane == row + (z % 2) * 64 + at, own, 0.0)
    own = jnp.sum(own, axis=1, keepdims=True)
    for yl in range(YL):
        for q in range(4):
            for pair in range(2):
                low, high = tiles[2 * pair, yl, q] * own, tiles[2 * pair + 1, yl, q] * own
                even = jnp.where(lane < 64, low, pltpu.roll(high, 64, 1))
                odd = jnp.where(lane < 64, pltpu.roll(low, 64, 1), high)
                start = yl * 2048 + q * 512 + pair * 128
                out_ref[:, start:start + 128] = even
                out_ref[:, start + 256:start + 384] = odd


def finish(place, whole):
    return pl.pallas_call(
        finish_kernel,
        out_shape=jax.ShapeDtypeStruct((8, 4096), jnp.float32),
        in_specs=[SMEM, VMEM],
        out_specs=VMEM,
        scratch_shapes=[pltpu.VMEM((XS * YL, 4, 128), jnp.float32)],
        compiler_params=PARAMS,
        cost_estimate=pl.CostEstimate(flops=262144, bytes_accessed=786432, transcendentals=4096),
    )(place, whole)


def shards(grads, second_moment):
    ex, feat = lax.axis_index("ex"), lax.axis_index("feat")
    z, y_lo = ex % ZS, ex // ZS
    x, y_hi, core = feat // (YH * CS), (feat // CS) % YH, feat % CS

    scaled, copies = scale(grads, second_moment)
    swapped = lax.all_to_all(scaled.reshape(XS, 64, 256), "feat", 0, 0, axis_index_groups=X_GROUPS, tiled=True)
    piece = jnp.transpose(swapped, (1, 0, 2)).reshape(64, XS * 256)
    left = lax.all_to_all(copies, AXES, 0, 0, axis_index_groups=LEFT_GROUPS, tiled=True)
    right = ring(piece, z, 1 - 2 * core)

    theirs, tile, right = half_product(1 - core, left, right)
    theirs = shift(theirs, lambda x, y, z, c: (x, y, z, c + 1))
    mine = half_product(core, left, right, tile) + theirs
    whole = lax.all_to_all(mine, AXES, 0, 0, axis_index_groups=XY_GROUPS, tiled=True)
    return finish(jnp.stack([x, y_lo, z, y_hi * 16 + core * 8]), whole)


def solution(mesh):
    return jax.shard_map(
        shards,
        mesh=mesh,
        in_specs=(P("ex", "feat"), P("feat")),
        out_specs=P(("ex", "feat"), None),
        check_vma=False,
    )
```
